32 devices in a mesh: grp: 2 (over x), row: 16 (over z, y, core).
Axes of the slice: x: 2, y: 2, z: 4, core: 2. Of those that a mesh axis runs over, the one named last changes fastest.
Arguments:
- right_sides: float32 [32, 512, 512], P(None, ('grp', 'row')), parts along dimension 1, may hold values from -180 to 180
- kappa_sq: float32 [512, 512], P(('grp', 'row')), parts along dimension 0, may hold values from 0.02 to 1
- inv_mass: float32 [512, 512], P(('grp', 'row')), parts along dimension 0, may hold values from 0.25 to 4
- cell_mask: int32 [512, 512], P(('grp', 'row')), parts along dimension 0, may hold values 0 or 1
- weights: bfloat16 [256, 8, 128, 512], P(('grp', 'row')), parts along dimension 0, may hold values from -0.75 to 0.75
- obs_precision: float32 [256, 128], P(('grp', 'row')), parts along dimension 0, may hold values from 0.5 to 8
- footprint: int32 [256, 8], P(('grp', 'row')), parts along dimension 0, may hold values from 0 to 255, as said below
Outputs:
- solution: float32 [32, 512, 512], P(None, ('grp', 'row')), parts along dimension 1
- residual: float32 [32, 512, 512], P(None, ('grp', 'row')), parts along dimension 1
The draws below stay inside these ranges and needn't reach their ends.
There are 2 independent parts, one for each index of `grp`. The reference program is written for one: setup_inputs(seed, part) draws one part's arguments, and reference() takes and returns one part's arrays. A program takes and returns all parts, laid end to end along the dimension named above; each array names one. Nothing has to cross between parts.
Inputs may be any that keep to these rules, and one draw needn't show every extreme that they name: Tile t's footprint rows lie in the rows 16 * (t // 8) - 16 to 16 * (t // 8) + 2 * 16 - 1; rows may repeat.
All inputs are finite; a program needn't handle non-finite values. No bound on the sum of `cell_mask` on one device may be relied on, other than what follows from the above.
Results may differ from the reference program's by a relative error of at most 0.0095.
Values may be sent and summed in bfloat16 or wider, within the bound.
A program may use at most 64 MiB of HBM per device.

```python
import math
import jax
import jax.numpy as jnp
from jax import lax

NRHS = 32
CR = 16
W = 512
TILES_DEV = 8
FP = 8
OB = 128
ITERS = 2
NR = 256
NTILES = 128


def draw_footprint(key, part):
    key = jax.random.fold_in(key, 5)
    offsets = jax.random.randint(key, (NTILES, FP), 0, 3 * CR)
    owners = jnp.arange(NTILES, dtype=jnp.int32) // TILES_DEV
    picked = jnp.clip(owners[:, None] * CR - CR + offsets, 0, NR - 1)
    picked = picked.at[0, 0].set(0)
    picked = picked.at[NTILES - 1, FP - 1].set(NR - 1)
    return picked.astype(jnp.int32)


def place_ends(drawn, rng, smallest, top_value):
    index_at = [jax.random.randint(jax.random.fold_in(rng, axis), (), 0, length) for axis, length in enumerate(drawn.shape)]
    main_axis = drawn.shape.index(max(drawn.shape))
    next_to = index_at[:main_axis] + [(index_at[main_axis] + 1) % drawn.shape[main_axis]] + index_at[main_axis + 1:]
    return drawn.at[tuple(index_at)].set(smallest).at[tuple(next_to)].set(top_value)


def shard_levels(own_key, dims, shards, smallest, high):
    def one(position, shards_of):
        draws = jax.random.uniform(jax.random.fold_in(jax.random.fold_in(own_key, 6), position), (shards_of,), jnp.float32, smallest / len(shards), high / len(shards))
        return jnp.repeat(jnp.exp(draws), dims[position] // shards_of).reshape((-1,) + (1,) * (len(dims) - position - 1))

    loudness = one(*shards[0])
    for cut in shards[1:]:
        loudness = loudness * one(*cut)
    return loudness


def centred(key, extent, scale, bound, shards=(), kind=jnp.bfloat16):
    values = jax.random.normal(key, extent, jnp.float32) * scale
    if len(shards) > 0:
        values = shard_levels(key, extent, shards, -0.22, 0.18) * values
    return jnp.clip(values, min=-bound, max=bound).astype(kind)


def setup_inputs(seed: int = 0, part: int = 0) -> dict:
    key_list = jax.random.split(jax.random.key(seed), 8)
    own_keys = jax.random.split(jax.random.fold_in(key_list[7], part), 8)
    right_sides = centred(own_keys[0], (NRHS, NR, W), 30.0, 180.0, ((1, 16),), jnp.float32)
    kappa_sq = jnp.clip(jnp.exp(math.log(1.0) - 3.912023 * jax.random.uniform(own_keys[1], (NR, W), jnp.float32) ** shard_levels(own_keys[1], (NR, W), ((0, 16),), -0.2, 0.2)), 0.02, 1.0)
    inv_mass = jnp.clip(jnp.exp(math.log(4.0) - 2.7725887 * jax.random.uniform(own_keys[2], (NR, W), jnp.float32) ** shard_levels(own_keys[2], (NR, W), ((0, 16),), -0.2, 0.2)), 0.25, 4.0)
    cell_mask = place_ends((jax.random.randint(own_keys[3], (NR, W), 0, 8) < 7).astype(jnp.int32), jax.random.fold_in(own_keys[3], 1), 0, 1)
    weights = centred(own_keys[4], (NTILES, FP, OB, W), (FP * W // 64) ** -0.5, 0.75, ((0, 16),))
    obs_precision = jnp.clip(jnp.exp(math.log(8.0) - 2.7725887 * jax.random.uniform(own_keys[5], (NTILES, OB), jnp.float32) ** shard_levels(own_keys[5], (NTILES, OB), ((0, 16),), -0.2, 0.2)), 0.5, 8.0)
    footprint = draw_footprint(jax.random.fold_in(jax.random.fold_in(key_list[7], part), 71), part)
    return {"right_sides": right_sides, "kappa_sq": kappa_sq, "inv_mass": inv_mass, "cell_mask": cell_mask, "weights": weights, "obs_precision": obs_precision, "footprint": footprint}


def stencil(field, kappa_sq, maskf):
    masked = maskf * field
    padded = jnp.pad(masked, ((0, 0), (1, 1), (1, 1)))
    beside_all = padded[:, 2:, 1:-1] + padded[:, :-2, 1:-1] + padded[:, 1:-1, 2:] + padded[:, 1:-1, :-2]
    return kappa_sq * field + maskf * (4.0 * field - beside_all)

def observe(field, weights, obs_precision, footprint):
    rounded = lax.optimization_barrier(field.astype(jnp.bfloat16)).astype(jnp.float32)

    def visit(total, item):
        tile_weights, tile_rows, tile_prec = item
        wide = tile_weights.astype(jnp.float32)
        picked = rounded[:, tile_rows, :]
        observed = jnp.einsum('kfc,foc->ko', picked, wide, precision=lax.Precision.HIGHEST)
        scaled = lax.optimization_barrier((tile_prec[None, :] * observed).astype(jnp.bfloat16)).astype(jnp.float32)
        adjoint = jnp.einsum('ko,foc->kfc', scaled, wide, precision=lax.Precision.HIGHEST)
        return (total.at[:, tile_rows, :].add(adjoint), None)
    total, unused = lax.scan(visit, jnp.zeros(field.shape, jnp.float32), (weights, footprint, obs_precision))
    return total

def gram_matrix(left, right):
    count = left.shape[0]
    return jnp.dot(left.reshape(count, -1), right.reshape(count, -1).T, precision=lax.Precision.HIGHEST)

def solve_small(matrix, target):
    factor = jnp.linalg.cholesky(0.5 * (matrix + matrix.T))
    return jax.scipy.linalg.cho_solve((factor, True), target)

def combine(coeffs, fields):
    return jnp.einsum('jk,jrc->krc', coeffs, fields, precision=lax.Precision.HIGHEST)

def reference(right_sides, kappa_sq, inv_mass, cell_mask, weights, obs_precision, footprint):
    maskf = cell_mask.astype(jnp.float32)

    def apply_precision(field):
        inner = stencil(field, kappa_sq, maskf)
        return stencil(inv_mass * inner, kappa_sq, maskf) + observe(field, weights, obs_precision, footprint)
    solution = jnp.zeros_like(right_sides)
    residual = right_sides
    direction = right_sides
    res_gram = gram_matrix(residual, residual)
    for step in range(ITERS):
        image = apply_precision(direction)
        step_size = solve_small(gram_matrix(direction, image), res_gram)
        solution = solution + combine(step_size, direction)
        residual = residual - combine(step_size, image)
        if step + 1 < ITERS:
            new_gram = gram_matrix(residual, residual)
            update_mix = solve_small(res_gram, new_gram)
            direction = residual + combine(update_mix, direction)
            res_gram = new_gram
    return (solution, residual)
```

```python
import functools

import jax
import jax.numpy as jnp
from jax import lax
from jax.experimental import pallas as pl
from jax.experimental.pallas import tpu as pltpu
from jax.sharding import PartitionSpec as P

RADIX = 4
HIGHEST = lax.Precision.HIGHEST
NN = (((1,), (0,)), ((), ()))
NT = (((1,), (1,)), ((), ()))
FIELD_EDGE, HALO, INNER_EDGE, TERMS = range(4)


def radices(n):
    out, stride = [], 1
    while stride < n:
        radix = RADIX if (n // stride) % RADIX == 0 else n // stride
        out.append((stride, radix))
        stride *= radix
    return out


def dot(a, b, dims=NN, precision=HIGHEST):
    return lax.dot_general(a, b, dims, precision=precision, preferred_element_type=jnp.float32)


def eliminate(mats):
    k = mats[0].shape[0]
    row_id = lax.broadcasted_iota(jnp.int32, mats[0].shape, 0)
    for i in range(k):
        new = []
        for a in mats:
            row = a[i : i + 1, :] * (1.0 / a[i : i + 1, i : i + 1])
            new.append(jnp.where(row_id == i, row, a - a[:, i : i + 1] * row))
        mats = new
    return mats


def kernel(
    n,
    rhs_ref, kap_ref, inv_ref, mask_ref, w_hbm, prec_ref, idx_ref,
    sol_ref, res_ref,
    w, ext, adj, sc, masked, img, image2, dirn, es, er, ts, tr, ar, aug,
    wsem, send_sem, recv_sem, ar_send, ar_recv,
):
    rows, nk, cols = rhs_ref.shape
    tiles, foot, obs, _ = w.shape
    picks = tiles * foot
    me = lax.axis_index("row")
    has_up, has_down = me > 0, me < n - 1
    levels = radices(n)

    for t in range(tiles):
        pltpu.make_async_copy(w_hbm.at[t], w.at[t], wsem.at[t]).start()

    def neighbour(d):
        return {"row": lax.rem(me + (1 if d == 0 else n - 1), n)}

    def partner(stride, radix, d):
        q = lax.rem(me // stride, radix)
        return {"row": me + (lax.rem(q + d, radix) - q) * stride}

    barrier = pltpu.get_barrier_semaphore()

    def greet(device):
        pl.semaphore_signal(barrier, inc=1, device_id=device, device_id_type=pl.DeviceIdType.MESH)

    count = 0
    for stride, radix in levels:
        for d in range(1, radix):
            greet(partner(stride, radix, d))
            count += 1
    pl.when(has_down)(lambda: greet(neighbour(0)))
    pl.when(has_up)(lambda: greet(neighbour(1)))

    def copy(it, kind, d, src, dst):
        return pltpu.make_async_remote_copy(
            src_ref=src,
            dst_ref=dst,
            send_sem=send_sem.at[it, kind, d],
            recv_sem=recv_sem.at[it, kind, d],
            device_id=neighbour(d),
            device_id_type=pl.DeviceIdType.MESH,
        )

    sends = (has_down, has_up)
    receives = (has_up, has_down)

    def pair(it, kind):
        if kind == HALO:
            own = ext.at[it, pl.ds(rows, rows)]
            return (
                copy(it, kind, 0, own, ext.at[it, pl.ds(0, rows)]),
                copy(it, kind, 1, own, ext.at[it, pl.ds(2 * rows, rows)]),
            )
        if kind == TERMS:
            return tuple(copy(it, kind, d, ts.at[it, d], tr.at[it, d]) for d in range(2))
        e = 0 if kind == FIELD_EDGE else 1
        return tuple(copy(it, kind, d, es.at[it, e, d], er.at[it, e, d]) for d in range(2))

    def start(it, kind):
        for d, c in enumerate(pair(it, kind)):
            pl.when(sends[d])(c.start)

    def arrive(it, kind):
        for d, c in enumerate(pair(it, kind)):
            pl.when(receives[d])(c.wait_recv)

    def drain(it, kind):
        for d, c in enumerate(pair(it, kind)):
            pl.when(sends[d])(c.wait_send)

    @pl.when(jnp.logical_not(has_up))
    def _():
        for it in range(2):
            ext[it, pl.ds(0, rows)] = jnp.zeros((rows, nk, cols), jnp.bfloat16)
            tr[it, 0] = jnp.zeros((rows, nk, cols), jnp.bfloat16)
            for e in range(2):
                er[it, e, 0] = jnp.zeros((nk, cols), jnp.bfloat16)

    @pl.when(jnp.logical_not(has_down))
    def _():
        for it in range(2):
            ext[it, pl.ds(2 * rows, rows)] = jnp.zeros((rows, nk, cols), jnp.bfloat16)
            tr[it, 1] = jnp.zeros((rows, nk, cols), jnp.bfloat16)
            for e in range(2):
                er[it, e, 1] = jnp.zeros((nk, cols), jnp.bfloat16)

    adj[0] = jnp.zeros((nk, cols), jnp.float32)

    lane = lax.broadcasted_iota(jnp.int32, (nk, cols), 1)
    maskf = mask_ref[...].astype(jnp.float32)
    kap = kap_ref[...]
    inv = inv_ref[...]

    def at(table, r):
        return table[r : r + 1, :]

    def beside(r):
        m = masked[r + 1]
        right = jnp.where(lane == cols - 1, 0.0, pltpu.roll(m, cols - 1, 1))
        left = jnp.where(lane == 0, 0.0, pltpu.roll(m, 1, 1))
        return masked[r] + masked[r + 2] + right + left

    def stage_edges(it, e):
        for d, r in ((0, rows), (1, 1)):
            es[it, e, d] = masked[r].astype(jnp.bfloat16)

    def take_edges(it, e):
        masked[0] = er[it, e, 0].astype(jnp.float32)
        masked[rows + 1] = er[it, e, 1].astype(jnp.float32)

    def apply(it, field, out):
        for r in range(rows):
            masked[r + 1] = at(maskf, r) * field[r]
            ext[it, rows + r] = field[r].astype(jnp.bfloat16)
        stage_edges(it, 0)
        if it == 0:
            down, up = (jnp.where(x, 1, 0) for x in (has_down, has_up))
            pl.semaphore_wait(barrier, count + down + up)
        start(it, FIELD_EDGE)
        start(it, HALO)
        arrive(it, FIELD_EDGE)
        take_edges(it, 0)
        for r in range(rows):
            out[r] = at(kap, r) * field[r] + at(maskf, r) * (4.0 * field[r] - beside(r))
        for r in range(rows):
            out[r] = at(inv, r) * out[r]
            masked[r + 1] = at(maskf, r) * out[r]
        stage_edges(it, 1)
        start(it, INNER_EDGE)
        arrive(it, HALO)

        def observe(t, carry):
            if it == 0:
                pltpu.make_async_copy(w_hbm.at[t], w.at[t], wsem.at[t]).wait()
            total = jnp.zeros((nk, obs), jnp.float32)
            for j in range(foot):
                x = ext[it, idx_ref[t * foot + j]]
                total += dot(x, w[t, j], NT, None)
            sc[t] = (prec_ref[pl.ds(t, 1), :] * total).astype(jnp.bfloat16)
            return carry

        lax.fori_loop(0, tiles, observe, 0)

        def spread(t, carry):
            for j in range(foot):
                adj[1 + t * foot + j] = dot(sc[t], w[t, j], NN, None)
            return carry

        lax.fori_loop(0, tiles, spread, 0)

        def link(i, carry):
            adj[1 + i] = adj[1 + i] + adj[idx_ref[picks + i]]
            return carry

        lax.fori_loop(0, picks, link, 0)

        def stage(r, carry):
            ts[it, 1, r] = adj[idx_ref[2 * picks + r]].astype(jnp.bfloat16)
            ts[it, 0, r] = adj[idx_ref[2 * picks + 2 * rows + r]].astype(jnp.bfloat16)
            return carry

        lax.fori_loop(0, rows, stage, 0)
        start(it, TERMS)
        arrive(it, INNER_EDGE)
        take_edges(it, 1)
        for r in range(rows):
            prior = at(kap, r) * out[r] + at(maskf, r) * (4.0 * out[r] - beside(r))
            out[r] = prior + adj[idx_ref[2 * picks + rows + r]]
        arrive(it, TERMS)
        for r in range(rows):
            out[r] += tr[it, 0, r].astype(jnp.float32) + tr[it, 1, r].astype(jnp.float32)
        for kind in range(4):
            drain(it, kind)

    def grams(a, b):
        parts = [jnp.zeros((nk, nk), jnp.float32) for _ in range(4)]
        for r in range(rows):
            x, y = a[r], b[r]
            for p, (f, g) in enumerate(((x, x), (x, y), (y, x), (y, y))):
                parts[p] += dot(f, g, NT)
        return parts

    def reduce_all(which, parts):
        value = jnp.concatenate(parts, axis=1)
        for lv, (stride, radix) in enumerate(levels):
            q = lax.rem(me // stride, radix)
            ar[which, lv, q] = value
            copies = [
                pltpu.make_async_remote_copy(
                    src_ref=ar.at[which, lv, q],
                    dst_ref=ar.at[which, lv, q],
                    send_sem=ar_send.at[which, lv, d],
                    recv_sem=ar_recv.at[which, lv, d],
                    device_id=partner(stride, radix, d),
                    device_id_type=pl.DeviceIdType.MESH,
                )
                for d in range(1, radix)
            ]
            for c in copies:
                c.start()
            for c in copies:
                c.wait_recv()
            for c in copies:
                c.wait_send()
            value = ar[which, lv, 0]
            for p in range(1, radix):
                value = value + ar[which, lv, p]
        return [value[:, p * nk : (p + 1) * nk] for p in range(4)]

    eye = (
        lax.broadcasted_iota(jnp.int32, (nk, nk), 0) == lax.broadcasted_iota(jnp.int32, (nk, nk), 1)
    ).astype(jnp.float32)
    pad = jnp.zeros((nk, 2 * nk), jnp.float32)

    def flipped(x):
        return dot(eye, x, NT)

    apply(0, rhs_ref, img)
    g00, g01, g10, g11 = reduce_all(0, grams(rhs_ref, img))
    first, second = eliminate(
        [
            jnp.concatenate([0.5 * (g01 + g10), g00, pad], axis=1),
            jnp.concatenate([g00, eye, pad], axis=1),
        ]
    )
    step = first[:, nk : 2 * nk]
    step_t = flipped(step)
    cross = dot(g01, step)
    new_gram = g00 - cross - flipped(cross) + dot(step_t, dot(g11, step))
    mix = dot(second[:, nk : 2 * nk], new_gram)
    mix_t = flipped(mix)
    for r in range(rows):
        b = rhs_ref[r]
        both = dot(jnp.concatenate([step_t, mix_t], axis=0), b)
        left = b - dot(step_t, img[r])
        sol_ref[r] = both[:nk]
        res_ref[r] = left
        dirn[r] = left + both[nk:]

    apply(1, dirn, image2)
    _, g01, g10, _ = reduce_all(1, grams(dirn, image2))
    (third,) = eliminate([jnp.concatenate([0.5 * (g01 + g10), new_gram, pad], axis=1)])
    step_t = flipped(third[:, nk : 2 * nk])
    for r in range(rows):
        sol_ref[r] += dot(step_t, dirn[r])
        res_ref[r] -= dot(step_t, image2[r])


def body(right_sides, kappa_sq, inv_mass, cell_mask, weights, obs_precision, footprint):
    nk, rows, cols = right_sides.shape
    tiles, foot, obs, _ = weights.shape
    picks = tiles * foot
    n = lax.axis_size("row")
    device = lax.axis_index("row")
    ids = (footprint - (device * rows - rows)).reshape(-1)
    wanted = jnp.concatenate([ids, jnp.arange(3 * rows, dtype=jnp.int32)])
    before = jnp.concatenate(
        [jnp.arange(picks, dtype=jnp.int32), jnp.full((3 * rows,), picks, jnp.int32)]
    )
    order = jnp.arange(picks, dtype=jnp.int32)
    same = (wanted[:, None] == ids[None, :]) & (order[None, :] < before[:, None])
    last = jnp.max(jnp.where(same, order[None, :] + 1, 0), axis=1)
    index = jnp.concatenate([ids, last])

    levels = len(radices(n))
    field = (rows, nk, cols)
    vmem = pl.BlockSpec(memory_space=pltpu.VMEM)
    f32, bf16 = jnp.float32, jnp.bfloat16
    solved, left = pl.pallas_call(
        functools.partial(kernel, n),
        out_shape=[jax.ShapeDtypeStruct(field, f32)] * 2,
        in_specs=[vmem] * 4
        + [pl.BlockSpec(memory_space=pl.ANY), vmem, pl.BlockSpec(memory_space=pltpu.SMEM)],
        out_specs=[vmem] * 2,
        scratch_shapes=[
            pltpu.VMEM(weights.shape, bf16),
            pltpu.VMEM((2, 3 * rows, nk, cols), bf16),
            pltpu.VMEM((picks + 1, nk, cols), f32),
            pltpu.VMEM((tiles, nk, obs), bf16),
            pltpu.VMEM((rows + 2, nk, cols), f32),
            pltpu.VMEM(field, f32),
            pltpu.VMEM(field, f32),
            pltpu.VMEM(field, f32),
            pltpu.VMEM((2, 2, 2, nk, cols), bf16),
            pltpu.VMEM((2, 2, 2, nk, cols), bf16),
            pltpu.VMEM((2, 2) + field, bf16),
            pltpu.VMEM((2, 2) + field, bf16),
            pltpu.VMEM((2, levels, RADIX, nk, 4 * nk), f32),
            pltpu.VMEM((2, nk, 4 * nk), f32),
            pltpu.SemaphoreType.DMA((tiles,)),
            pltpu.SemaphoreType.DMA((2, 4, 2)),
            pltpu.SemaphoreType.DMA((2, 4, 2)),
            pltpu.SemaphoreType.DMA((2, levels, RADIX)),
            pltpu.SemaphoreType.DMA((2, levels, RADIX)),
        ],
        compiler_params=pltpu.CompilerParams(
            collective_id=0, has_side_effects=True, vmem_limit_bytes=50 * 1024 * 1024
        ),
    )(
        jnp.swapaxes(right_sides, 0, 1),
        kappa_sq,
        inv_mass,
        cell_mask,
        weights,
        obs_precision,
        index,
    )
    return (jnp.swapaxes(solved, 0, 1), jnp.swapaxes(left, 0, 1))


def solution(mesh):
    placed = (
        P(None, ("grp", "row"), None),
        P(("grp", "row"), None),
        P(("grp", "row"), None),
        P(("grp", "row"), None),
        P(("grp", "row"), None, None, None),
        P(("grp", "row"), None),
        P(("grp", "row"), None),
    )
    return jax.shard_map(
        body,
        mesh=mesh,
        in_specs=placed,
        out_specs=(P(None, ("grp", "row"), None), P(None, ("grp", "row"), None)),
        check_vma=False,
    )
```

```python
import functools

import jax
import jax.numpy as jnp
from jax import lax
from jax.experimental import pallas as pl
from jax.experimental.pallas import tpu as pltpu
from jax.sharding import PartitionSpec as P

RADIX = 16
HALVES = 2
HIGHEST = lax.Precision.HIGHEST
NN = (((1,), (0,)), ((), ()))
NT = (((1,), (1,)), ((), ()))
FIELD_EDGE, HALO, INNER_EDGE, TERMS = range(4)
KINDS = TERMS + HALVES


def radices(n):
    out, stride = [], 1
    while stride < n:
        radix = min(RADIX, n // stride)
        out.append((stride, radix))
        stride *= radix
    return out


def dot(a, b, dims=NN, precision=HIGHEST):
    return lax.dot_general(a, b, dims, precision=precision, preferred_element_type=jnp.float32)


def eliminate(mats):
    k = mats[0].shape[0]
    row_id = lax.broadcasted_iota(jnp.int32, mats[0].shape, 0)
    for i in range(k):
        new = []
        for a in mats:
            row = a[i : i + 1, :] * (1.0 / a[i : i + 1, i : i + 1])
            new.append(jnp.where(row_id == i, row, a - a[:, i : i + 1] * row))
        mats = new
    return mats


def kernel(
    n,
    rhs_ref, kap_hbm, inv_hbm, mask_hbm, w_hbm, prec_hbm, idx_ref,
    sol_ref, res_ref,
    w, ext, adj, sc, masked, img, image2, dirn, es, er, ts, tr, ar0, ar1, packed,
    kap_ref, inv_ref, mask_ref, prec_ref, tsem, wsem, send_sem, recv_sem, ar_send, ar_recv,
):
    rows, nk, cols = rhs_ref.shape
    tiles, foot, obs, _ = w.shape
    picks = tiles * foot
    me = lax.axis_index("row")
    has_up, has_down = me > 0, me < n - 1
    levels = radices(n)

    half = cols // HALVES
    tables = [
        pltpu.make_async_copy(src, dst, tsem.at[i])
        for i, (src, dst) in enumerate(
            ((kap_hbm, kap_ref), (inv_hbm, inv_ref), (mask_hbm, mask_ref), (prec_hbm, prec_ref))
        )
    ]
    for c in tables:
        c.start()
    for t in range(tiles):
        pltpu.make_async_copy(w_hbm.at[t], w.at[t], wsem.at[t]).start()

    def neighbour(d):
        return {"row": lax.rem(me + (1 if d == 0 else n - 1), n)}

    def partner(stride, radix, d):
        q = lax.rem(me // stride, radix)
        return {"row": me + (lax.rem(q + d, radix) - q) * stride}

    barrier = pltpu.get_barrier_semaphore()

    def greet(device):
        pl.semaphore_signal(barrier, inc=1, device_id=device, device_id_type=pl.DeviceIdType.MESH)

    count = 0
    for stride, radix in levels:
        for d in range(1, radix):
            greet(partner(stride, radix, d))
            count += 1
    pl.when(has_down)(lambda: greet(neighbour(0)))
    pl.when(has_up)(lambda: greet(neighbour(1)))

    def copy(it, kind, d, src, dst):
        return pltpu.make_async_remote_copy(
            src_ref=src,
            dst_ref=dst,
            send_sem=send_sem.at[it, kind, d],
            recv_sem=recv_sem.at[it, kind, d],
            device_id=neighbour(d),
            device_id_type=pl.DeviceIdType.MESH,
        )

    sends = (has_down, has_up)
    receives = (has_up, has_down)

    def pair(it, kind):
        if kind == HALO:
            own = ext.at[it, pl.ds(rows, rows)]
            return (
                copy(it, kind, 0, own, ext.at[it, pl.ds(0, rows)]),
                copy(it, kind, 1, own, ext.at[it, pl.ds(2 * rows, rows)]),
            )
        if kind >= TERMS:
            h = kind - TERMS
            return tuple(copy(it, kind, d, ts.at[it, h, d], tr.at[it, h, d]) for d in range(2))
        e = 0 if kind == FIELD_EDGE else 1
        return tuple(copy(it, kind, d, es.at[it, e, d], er.at[it, e, d]) for d in range(2))

    def start(it, kind):
        for d, c in enumerate(pair(it, kind)):
            pl.when(sends[d])(c.start)

    def arrive(it, kind):
        for d, c in enumerate(pair(it, kind)):
            pl.when(receives[d])(c.wait_recv)

    def drain(it, kind):
        for d, c in enumerate(pair(it, kind)):
            pl.when(sends[d])(c.wait_send)

    @pl.when(jnp.logical_not(has_up))
    def _():
        for it in range(2):
            ext[it, pl.ds(0, rows)] = jnp.zeros((rows, nk, cols), jnp.bfloat16)
            for h in range(HALVES):
                tr[it, h, 0] = jnp.zeros((rows, nk, half), jnp.bfloat16)
            for e in range(2):
                er[it, e, 0] = jnp.zeros((nk, cols), jnp.bfloat16)

    @pl.when(jnp.logical_not(has_down))
    def _():
        for it in range(2):
            ext[it, pl.ds(2 * rows, rows)] = jnp.zeros((rows, nk, cols), jnp.bfloat16)
            for h in range(HALVES):
                tr[it, h, 1] = jnp.zeros((rows, nk, half), jnp.bfloat16)
            for e in range(2):
                er[it, e, 1] = jnp.zeros((nk, cols), jnp.bfloat16)

    for h in range(HALVES):
        adj[h, 0] = jnp.zeros((nk, half), jnp.float32)
    for c in tables:
        c.wait()

    lane = lax.broadcasted_iota(jnp.int32, (nk, cols), 1)
    maskf = mask_ref[...].astype(jnp.float32)
    kap = kap_ref[...]
    inv = inv_ref[...]

    def at(table, r):
        return table[r : r + 1, :]

    def beside(r):
        m = masked[r + 1]
        right = jnp.where(lane == cols - 1, 0.0, pltpu.roll(m, cols - 1, 1))
        left = jnp.where(lane == 0, 0.0, pltpu.roll(m, 1, 1))
        return masked[r] + masked[r + 2] + right + left

    def stage_edges(it, e):
        for d, r in ((0, rows), (1, 1)):
            es[it, e, d] = masked[r].astype(jnp.bfloat16)

    def take_edges(it, e):
        masked[0] = er[it, e, 0].astype(jnp.float32)
        masked[rows + 1] = er[it, e, 1].astype(jnp.float32)

    def apply(it, field, out):
        for r in range(rows):
            masked[r + 1] = at(maskf, r) * field[r]
            ext[it, rows + r] = field[r].astype(jnp.bfloat16)
        stage_edges(it, 0)
        if it == 0:
            down, up = (jnp.where(x, 1, 0) for x in (has_down, has_up))
            pl.semaphore_wait(barrier, count + down + up)
        start(it, FIELD_EDGE)
        start(it, HALO)
        arrive(it, FIELD_EDGE)
        take_edges(it, 0)
        for r in range(rows):
            out[r] = at(kap, r) * field[r] + at(maskf, r) * (4.0 * field[r] - beside(r))
        for r in range(rows):
            out[r] = at(inv, r) * out[r]
            masked[r + 1] = at(maskf, r) * out[r]
        stage_edges(it, 1)
        start(it, INNER_EDGE)
        arrive(it, HALO)

        def observe(t, carry):
            if it == 0:
                pltpu.make_async_copy(w_hbm.at[t], w.at[t], wsem.at[t]).wait()
            total = jnp.zeros((nk, obs), jnp.float32)
            for j in range(foot):
                x = ext[it, idx_ref[t * foot + j]]
                total += dot(x, w[t, j], NT, None)
            sc[t] = (prec_ref[pl.ds(t, 1), :] * total).astype(jnp.bfloat16)
            return carry

        lax.fori_loop(0, tiles, observe, 0, unroll=2)

        for h in range(HALVES):
            part = pl.ds(h * half, half)

            def spread(t, carry):
                for j in range(foot):
                    adj[h, 1 + t * foot + j] = dot(sc[t], w[t, j, :, part], NN, None)
                return carry

            lax.fori_loop(0, tiles, spread, 0, unroll=2)

            def link(i, carry):
                adj[h, 1 + i] = adj[h, 1 + i] + adj[h, idx_ref[picks + i]]
                return carry

            lax.fori_loop(0, picks, link, 0, unroll=4)

            def stage(r, carry):
                ts[it, h, 1, r] = adj[h, idx_ref[2 * picks + r]].astype(jnp.bfloat16)
                ts[it, h, 0, r] = adj[h, idx_ref[2 * picks + 2 * rows + r]].astype(jnp.bfloat16)
                return carry

            lax.fori_loop(0, rows, stage, 0, unroll=4)
            start(it, TERMS + h)
        arrive(it, INNER_EDGE)
        take_edges(it, 1)
        for r in range(rows):
            out[r] = at(kap, r) * out[r] + at(maskf, r) * (4.0 * out[r] - beside(r))
        for h in range(HALVES):
            part = pl.ds(h * half, half)
            arrive(it, TERMS + h)
            for r in range(rows):
                beyond = tr[it, h, 0, r].astype(jnp.float32) + tr[it, h, 1, r].astype(jnp.float32)
                out[r, :, part] += adj[h, idx_ref[2 * picks + rows + r]] + beyond
        for kind in range(KINDS):
            drain(it, kind)

    def halves_of(x):
        high = x.astype(jnp.bfloat16)
        return high, (x - high.astype(jnp.float32)).astype(jnp.bfloat16)

    def pack(a, b):
        total = jnp.zeros((4 * nk, 4 * nk), jnp.float32)
        for r in range(rows):
            a_high, a_low = halves_of(a[r])
            b_high, b_low = halves_of(b[r])
            x = jnp.concatenate([a_high, b_high, a_low, b_low], axis=0)
            packed[r] = x
            total += dot(x, x, NT, None)
        total = total[: 2 * nk] + total[2 * nk :]
        return total[:, : 2 * nk] + total[:, 2 * nk :]

    def combine(coeffs):
        high, low = halves_of(coeffs)
        wide = jnp.concatenate([high, high, low], axis=1)

        def row(r):
            x = packed[r]
            return dot(wide, jnp.concatenate([x, x[: 2 * nk]], axis=0), NN, None)

        return row

    def reduce_all(which, ar, value):
        for lv, (stride, radix) in enumerate(levels):
            q = lax.rem(me // stride, radix)
            ar[lv, q] = value
            copies = [
                pltpu.make_async_remote_copy(
                    src_ref=ar.at[lv, q],
                    dst_ref=ar.at[lv, q],
                    send_sem=ar_send.at[which, lv, d],
                    recv_sem=ar_recv.at[which, lv, d],
                    device_id=partner(stride, radix, d),
                    device_id_type=pl.DeviceIdType.MESH,
                )
                for d in range(1, radix)
            ]
            for c in copies:
                c.start()
            for c in copies:
                c.wait_recv()
            for c in copies:
                c.wait_send()
            value = ar[lv, 0]
            for p in range(1, radix):
                value = value + ar[lv, p]
        return value

    eye = (
        lax.broadcasted_iota(jnp.int32, (nk, nk), 0) == lax.broadcasted_iota(jnp.int32, (nk, nk), 1)
    ).astype(jnp.float32)
    pad = jnp.zeros((nk, 2 * nk), jnp.float32)

    def flipped(x):
        return dot(eye, x, NT)

    apply(0, rhs_ref, img)
    total = pack(rhs_ref, img)
    total = reduce_all(0, ar0, jnp.concatenate([total[:nk], total[nk:]], axis=1))
    g00, g01, g10, g11 = (total[:, p * nk : (p + 1) * nk] for p in range(4))
    first, second = eliminate(
        [
            jnp.concatenate([0.5 * (g01 + g10), g00, pad], axis=1),
            jnp.concatenate([g00, eye, pad], axis=1),
        ]
    )
    step = first[:, nk : 2 * nk]
    step_t = flipped(step)
    new_gram = g00 - dot(g01, step) - dot(step_t, g10 - dot(g11, step))
    mix_t = dot(new_gram, second[:, nk : 2 * nk])
    none = jnp.zeros((nk, nk), jnp.float32)
    rows_of = combine(
        jnp.concatenate(
            [
                jnp.concatenate([step_t, none], axis=1),
                jnp.concatenate([none, step_t], axis=1),
                jnp.concatenate([mix_t, none], axis=1),
            ],
            axis=0,
        )
    )
    for r in range(rows):
        all_three = rows_of(r)
        left = rhs_ref[r] - all_three[nk : 2 * nk]
        sol_ref[r] = all_three[:nk]
        res_ref[r] = left
        dirn[r] = left + all_three[2 * nk :]

    apply(1, dirn, image2)
    total = pack(dirn, image2)
    total = 0.5 * (total[:nk, nk:] + total[nk:, :nk])
    fold = nk // 4
    total = jnp.concatenate([total[p * fold : (p + 1) * fold] for p in range(4)], axis=1)
    total = reduce_all(1, ar1, total)
    total = jnp.concatenate([total[:, p * nk : (p + 1) * nk] for p in range(4)], axis=0)
    (third,) = eliminate([jnp.concatenate([total, new_gram, pad], axis=1)])
    step_t = flipped(third[:, nk : 2 * nk])
    rows_of = combine(
        jnp.concatenate(
            [
                jnp.concatenate([step_t, none], axis=1),
                jnp.concatenate([none, step_t], axis=1),
            ],
            axis=0,
        )
    )
    for r in range(rows):
        both = rows_of(r)
        sol_ref[r] += both[:nk]
        res_ref[r] -= both[nk:]


def body(right_sides, kappa_sq, inv_mass, cell_mask, weights, obs_precision, footprint):
    nk, rows, cols = right_sides.shape
    tiles, foot, obs, _ = weights.shape
    picks = tiles * foot
    n = lax.axis_size("row")
    device = lax.axis_index("row")
    ids = (footprint - (device * rows - rows)).reshape(-1)
    wanted = jnp.concatenate([ids, jnp.arange(3 * rows, dtype=jnp.int32)])
    before = jnp.concatenate(
        [jnp.arange(picks, dtype=jnp.int32), jnp.full((3 * rows,), picks, jnp.int32)]
    )
    order = jnp.arange(picks, dtype=jnp.int32)
    same = (wanted[:, None] == ids[None, :]) & (order[None, :] < before[:, None])
    last = jnp.max(jnp.where(same, order[None, :] + 1, 0), axis=1)
    index = jnp.concatenate([ids, last])

    levels = len(radices(n))
    half = cols // HALVES
    field = (rows, nk, cols)
    vmem = pl.BlockSpec(memory_space=pltpu.VMEM)
    f32, bf16 = jnp.float32, jnp.bfloat16
    solved, left = pl.pallas_call(
        functools.partial(kernel, n),
        out_shape=[jax.ShapeDtypeStruct(field, f32)] * 2,
        in_specs=[vmem]
        + [pl.BlockSpec(memory_space=pl.ANY)] * 5
        + [pl.BlockSpec(memory_space=pltpu.SMEM)],
        out_specs=[vmem] * 2,
        scratch_shapes=[
            pltpu.VMEM(weights.shape, bf16),
            pltpu.VMEM((2, 3 * rows, nk, cols), bf16),
            pltpu.VMEM((HALVES, picks + 1, nk, half), f32),
            pltpu.VMEM((tiles, nk, obs), bf16),
            pltpu.VMEM((rows + 2, nk, cols), f32),
            pltpu.VMEM(field, f32),
            pltpu.VMEM(field, f32),
            pltpu.VMEM(field, f32),
            pltpu.VMEM((2, 2, 2, nk, cols), bf16),
            pltpu.VMEM((2, 2, 2, nk, cols), bf16),
            pltpu.VMEM((2, HALVES, 2, rows, nk, half), bf16),
            pltpu.VMEM((2, HALVES, 2, rows, nk, half), bf16),
            pltpu.VMEM((levels, RADIX, nk, 4 * nk), f32),
            pltpu.VMEM((levels, RADIX, nk // 4, 4 * nk), f32),
            pltpu.VMEM((rows, 4 * nk, cols), bf16),
            pltpu.VMEM(kappa_sq.shape, f32),
            pltpu.VMEM(inv_mass.shape, f32),
            pltpu.VMEM(cell_mask.shape, jnp.int32),
            pltpu.VMEM(obs_precision.shape, f32),
            pltpu.SemaphoreType.DMA((4,)),
            pltpu.SemaphoreType.DMA((tiles,)),
            pltpu.SemaphoreType.DMA((2, KINDS, 2)),
            pltpu.SemaphoreType.DMA((2, KINDS, 2)),
            pltpu.SemaphoreType.DMA((2, levels, RADIX)),
            pltpu.SemaphoreType.DMA((2, levels, RADIX)),
        ],
        compiler_params=pltpu.CompilerParams(
            collective_id=0, has_side_effects=True, vmem_limit_bytes=60 * 1024 * 1024
        ),
    )(
        jnp.swapaxes(right_sides, 0, 1),
        kappa_sq,
        inv_mass,
        cell_mask,
        weights,
        obs_precision,
        index,
    )
    return (jnp.swapaxes(solved, 0, 1), jnp.swapaxes(left, 0, 1))


def solution(mesh):
    placed = (
        P(None, ("grp", "row"), None),
        P(("grp", "row"), None),
        P(("grp", "row"), None),
        P(("grp", "row"), None),
        P(("grp", "row"), None, None, None),
        P(("grp", "row"), None),
        P(("grp", "row"), None),
    )
    return jax.shard_map(
        body,
        mesh=mesh,
        in_specs=placed,
        out_specs=(P(None, ("grp", "row"), None), P(None, ("grp", "row"), None)),
        check_vma=False,
    )
```

```python
import functools

import jax
import jax.numpy as jnp
from jax import lax
from jax.experimental import pallas as pl
from jax.experimental.pallas import tpu as pltpu
from jax.sharding import PartitionSpec as P

RADIX = 16
HALVES = 2
HIGHEST = lax.Precision.HIGHEST
NN = (((1,), (0,)), ((), ()))
NT = (((1,), (1,)), ((), ()))
FIELD_EDGE, HALO, INNER_EDGE, TERMS = range(4)
KINDS = TERMS + HALVES


def radices(n):
    out, stride = [], 1
    while stride < n:
        radix = min(RADIX, n // stride)
        out.append((stride, radix))
        stride *= radix
    return out


def dot(a, b, dims=NN, precision=HIGHEST):
    return lax.dot_general(a, b, dims, precision=precision, preferred_element_type=jnp.float32)


def eliminate(mats):
    k = mats[0].shape[0]
    row_id = lax.broadcasted_iota(jnp.int32, mats[0].shape, 0)
    for i in range(k):
        new = []
        for a in mats:
            row = a[i : i + 1, :] * (1.0 / a[i : i + 1, i : i + 1])
            new.append(jnp.where(row_id == i, row, a - a[:, i : i + 1] * row))
        mats = new
    return mats


def kernel(
    n,
    rhs_ref, kap_hbm, inv_hbm, mask_hbm, w_hbm, prec_hbm, idx_ref,
    sol_ref, res_ref,
    w, ext, adj, sc, masked, img, image2, dirn, es, er, ts, tr, vown, vhalo, ar0, ar1, packed,
    kap_ref, inv_ref, mask_ref, prec_ref, tsem, wsem, send_sem, recv_sem, ar_send, ar_recv,
):
    rows, nk, cols = rhs_ref.shape
    tiles, foot, obs, _ = w.shape
    picks = tiles * foot
    me = lax.axis_index("row")
    has_up, has_down = me > 0, me < n - 1
    levels = radices(n)

    half = cols // HALVES
    tables = [
        pltpu.make_async_copy(src, dst, tsem.at[i])
        for i, (src, dst) in enumerate(
            ((kap_hbm, kap_ref), (inv_hbm, inv_ref), (mask_hbm, mask_ref), (prec_hbm, prec_ref))
        )
    ]
    for c in tables:
        c.start()
    for t in range(tiles):
        pltpu.make_async_copy(w_hbm.at[t], w.at[t], wsem.at[t]).start()

    def neighbour(d):
        return {"row": lax.rem(me + (1 if d == 0 else n - 1), n)}

    def partner(stride, radix, d):
        q = lax.rem(me // stride, radix)
        return {"row": me + (lax.rem(q + d, radix) - q) * stride}

    barrier = pltpu.get_barrier_semaphore()

    def greet(device):
        pl.semaphore_signal(barrier, inc=1, device_id=device, device_id_type=pl.DeviceIdType.MESH)

    count = 0
    for stride, radix in levels:
        for d in range(1, radix):
            greet(partner(stride, radix, d))
            count += 1
    pl.when(has_down)(lambda: greet(neighbour(0)))
    pl.when(has_up)(lambda: greet(neighbour(1)))

    def copy(it, kind, d, src, dst):
        return pltpu.make_async_remote_copy(
            src_ref=src,
            dst_ref=dst,
            send_sem=send_sem.at[it, kind, d],
            recv_sem=recv_sem.at[it, kind, d],
            device_id=neighbour(d),
            device_id_type=pl.DeviceIdType.MESH,
        )

    sends = (has_down, has_up)
    receives = (has_up, has_down)

    def pair(it, kind):
        if kind == HALO:
            if it == 1:
                return tuple(copy(it, kind, d, vown, vhalo.at[d]) for d in range(2))
            own = ext.at[pl.ds(rows, rows)]
            return (
                copy(it, kind, 0, own, ext.at[pl.ds(0, rows)]),
                copy(it, kind, 1, own, ext.at[pl.ds(2 * rows, rows)]),
            )
        if kind >= TERMS:
            h = kind - TERMS
            return tuple(copy(it, kind, d, ts.at[it, h, d], tr.at[it, h, d]) for d in range(2))
        e = 0 if kind == FIELD_EDGE else 1
        return tuple(copy(it, kind, d, es.at[it, e, d], er.at[it, e, d]) for d in range(2))

    def start(it, kind):
        for d, c in enumerate(pair(it, kind)):
            pl.when(sends[d])(c.start)

    def arrive(it, kind):
        for d, c in enumerate(pair(it, kind)):
            pl.when(receives[d])(c.wait_recv)

    def drain(it, kind):
        for d, c in enumerate(pair(it, kind)):
            pl.when(sends[d])(c.wait_send)

    @pl.when(jnp.logical_not(has_up))
    def _():
        ext[pl.ds(0, rows)] = jnp.zeros((rows, nk, cols), jnp.bfloat16)
        vhalo[0] = jnp.zeros((rows, nk, cols), jnp.bfloat16)
        for it in range(2):
            for h in range(HALVES):
                tr[it, h, 0] = jnp.zeros((rows, nk, half), jnp.bfloat16)
            for e in range(2):
                er[it, e, 0] = jnp.zeros((nk, cols), jnp.bfloat16)

    @pl.when(jnp.logical_not(has_down))
    def _():
        ext[pl.ds(2 * rows, rows)] = jnp.zeros((rows, nk, cols), jnp.bfloat16)
        vhalo[1] = jnp.zeros((rows, nk, cols), jnp.bfloat16)
        for it in range(2):
            for h in range(HALVES):
                tr[it, h, 1] = jnp.zeros((rows, nk, half), jnp.bfloat16)
            for e in range(2):
                er[it, e, 1] = jnp.zeros((nk, cols), jnp.bfloat16)

    for h in range(HALVES):
        adj[h, 0] = jnp.zeros((nk, half), jnp.float32)
    for c in tables:
        c.wait()

    lane = lax.broadcasted_iota(jnp.int32, (nk, cols), 1)
    maskf = mask_ref[...].astype(jnp.float32)
    kap = kap_ref[...]
    inv = inv_ref[...]

    def at(table, r):
        return table[r : r + 1, :]

    def beside(r):
        m = masked[r + 1]
        right = jnp.where(lane == cols - 1, 0.0, pltpu.roll(m, cols - 1, 1))
        left = jnp.where(lane == 0, 0.0, pltpu.roll(m, 1, 1))
        return masked[r] + masked[r + 2] + right + left

    def stage_edges(it, e):
        for d, r in ((0, rows), (1, 1)):
            es[it, e, d] = masked[r].astype(jnp.bfloat16)

    def take_edges(it, e):
        masked[0] = er[it, e, 0].astype(jnp.float32)
        masked[rows + 1] = er[it, e, 1].astype(jnp.float32)

    def apply(it, field, out, make_halo=None):
        for r in range(rows):
            masked[r + 1] = at(maskf, r) * field[r]
            ext[rows + r] = field[r].astype(jnp.bfloat16)
        stage_edges(it, 0)
        if it == 0:
            down, up = (jnp.where(x, 1, 0) for x in (has_down, has_up))
            pl.semaphore_wait(barrier, count + down + up)
        start(it, FIELD_EDGE)
        if make_halo is None:
            start(it, HALO)
        else:
            make_halo()
        arrive(it, FIELD_EDGE)
        take_edges(it, 0)
        for r in range(rows):
            out[r] = at(kap, r) * field[r] + at(maskf, r) * (4.0 * field[r] - beside(r))
        for r in range(rows):
            out[r] = at(inv, r) * out[r]
            masked[r + 1] = at(maskf, r) * out[r]
        stage_edges(it, 1)
        start(it, INNER_EDGE)
        if make_halo is None:
            arrive(it, HALO)

        def observe(t, carry):
            if it == 0:
                pltpu.make_async_copy(w_hbm.at[t], w.at[t], wsem.at[t]).wait()
            total = jnp.zeros((nk, obs), jnp.float32)
            for j in range(foot):
                x = ext[idx_ref[t * foot + j]]
                total += dot(x, w[t, j], NT, None)
            sc[t] = (prec_ref[pl.ds(t, 1), :] * total).astype(jnp.bfloat16)
            return carry

        lax.fori_loop(0, tiles, observe, 0, unroll=2)

        for h in range(HALVES):
            part = pl.ds(h * half, half)

            def spread(t, carry):
                for j in range(foot):
                    adj[h, 1 + t * foot + j] = dot(sc[t], w[t, j, :, part], NN, None)
                return carry

            lax.fori_loop(0, tiles, spread, 0, unroll=2)

            def link(i, carry):
                adj[h, 1 + i] = adj[h, 1 + i] + adj[h, idx_ref[picks + i]]
                return carry

            lax.fori_loop(0, picks, link, 0, unroll=4)

            def stage(r, carry):
                ts[it, h, 1, r] = adj[h, idx_ref[2 * picks + r]].astype(jnp.bfloat16)
                ts[it, h, 0, r] = adj[h, idx_ref[2 * picks + 2 * rows + r]].astype(jnp.bfloat16)
                return carry

            lax.fori_loop(0, rows, stage, 0, unroll=4)
            start(it, TERMS + h)
        arrive(it, INNER_EDGE)
        take_edges(it, 1)
        for r in range(rows):
            out[r] = at(kap, r) * out[r] + at(maskf, r) * (4.0 * out[r] - beside(r))
        for h in range(HALVES):
            part = pl.ds(h * half, half)
            arrive(it, TERMS + h)
            for r in range(rows):
                beyond = tr[it, h, 0, r].astype(jnp.float32) + tr[it, h, 1, r].astype(jnp.float32)
                out[r, :, part] += adj[h, idx_ref[2 * picks + rows + r]] + beyond
        if it == 0:
            for r in range(rows):
                vown[r] = out[r].astype(jnp.bfloat16)
            start(1, HALO)
        for kind in range(KINDS):
            drain(it, kind)

    def halves_of(x):
        high = x.astype(jnp.bfloat16)
        return high, (x - high.astype(jnp.float32)).astype(jnp.bfloat16)

    def pack(a, b):
        total = jnp.zeros((4 * nk, 4 * nk), jnp.float32)
        for r in range(rows):
            a_high, a_low = halves_of(a[r])
            b_high, b_low = halves_of(b[r])
            x = jnp.concatenate([a_high, b_high, a_low, b_low], axis=0)
            packed[r] = x
            total += dot(x, x, NT, None)
        total = total[: 2 * nk] + total[2 * nk :]
        return total[:, : 2 * nk] + total[:, 2 * nk :]

    def combine(coeffs):
        high, low = halves_of(coeffs)
        wide = jnp.concatenate([high, high, low], axis=1)

        def row(r):
            x = packed[r]
            return dot(wide, jnp.concatenate([x, x[: 2 * nk]], axis=0), NN, None)

        return row

    def reduce_all(which, ar, value):
        for lv, (stride, radix) in enumerate(levels):
            q = lax.rem(me // stride, radix)
            ar[lv, q] = value
            copies = [
                pltpu.make_async_remote_copy(
                    src_ref=ar.at[lv, q],
                    dst_ref=ar.at[lv, q],
                    send_sem=ar_send.at[which, lv, d],
                    recv_sem=ar_recv.at[which, lv, d],
                    device_id=partner(stride, radix, d),
                    device_id_type=pl.DeviceIdType.MESH,
                )
                for d in range(1, radix)
            ]
            for c in copies:
                c.start()
            for c in copies:
                c.wait_recv()
            for c in copies:
                c.wait_send()
            value = ar[lv, 0]
            for p in range(1, radix):
                value = value + ar[lv, p]
        return value

    eye = (
        lax.broadcasted_iota(jnp.int32, (nk, nk), 0) == lax.broadcasted_iota(jnp.int32, (nk, nk), 1)
    ).astype(jnp.float32)
    pad = jnp.zeros((nk, 2 * nk), jnp.float32)

    def flipped(x):
        return dot(eye, x, NT)

    apply(0, rhs_ref, img)
    total = pack(rhs_ref, img)
    total = reduce_all(0, ar0, jnp.concatenate([total[:nk], total[nk:]], axis=1))
    g00, g01, g10, g11 = (total[:, p * nk : (p + 1) * nk] for p in range(4))
    first, second = eliminate(
        [
            jnp.concatenate([0.5 * (g01 + g10), g00, pad], axis=1),
            jnp.concatenate([g00, eye, pad], axis=1),
        ]
    )
    step = first[:, nk : 2 * nk]
    step_t = flipped(step)
    new_gram = g00 - dot(g01, step) - dot(step_t, g10 - dot(g11, step))
    mix_t = dot(new_gram, second[:, nk : 2 * nk])
    none = jnp.zeros((nk, nk), jnp.float32)
    rows_of = combine(
        jnp.concatenate(
            [
                jnp.concatenate([step_t, none], axis=1),
                jnp.concatenate([none, step_t], axis=1),
                jnp.concatenate([mix_t, none], axis=1),
            ],
            axis=0,
        )
    )
    for r in range(rows):
        all_three = rows_of(r)
        left = rhs_ref[r] - all_three[nk : 2 * nk]
        sol_ref[r] = all_three[:nk]
        res_ref[r] = left
        dirn[r] = left + all_three[2 * nk :]

    high, low = halves_of(jnp.concatenate([mix_t, -step_t], axis=1))
    beyond_t = jnp.concatenate([high, low], axis=1)

    def beyond_direction():
        arrive(1, HALO)
        for d in range(2):
            def one(r, carry):
                x = ext[2 * rows * d + r]
                y = vhalo[d, r]
                new = dot(beyond_t, jnp.concatenate([x, y, x, y], axis=0), NN, None)
                ext[2 * rows * d + r] = (x.astype(jnp.float32) + new).astype(jnp.bfloat16)
                return carry

            lax.fori_loop(0, rows, one, 0, unroll=4)

    apply(1, dirn, image2, beyond_direction)
    total = pack(dirn, image2)
    total = 0.5 * (total[:nk, nk:] + total[nk:, :nk])
    fold = nk // 4
    total = jnp.concatenate([total[p * fold : (p + 1) * fold] for p in range(4)], axis=1)
    total = reduce_all(1, ar1, total)
    total = jnp.concatenate([total[:, p * nk : (p + 1) * nk] for p in range(4)], axis=0)
    (third,) = eliminate([jnp.concatenate([total, new_gram, pad], axis=1)])
    step_t = flipped(third[:, nk : 2 * nk])
    rows_of = combine(
        jnp.concatenate(
            [
                jnp.concatenate([step_t, none], axis=1),
                jnp.concatenate([none, step_t], axis=1),
            ],
            axis=0,
        )
    )
    for r in range(rows):
        both = rows_of(r)
        sol_ref[r] += both[:nk]
        res_ref[r] -= both[nk:]


def body(right_sides, kappa_sq, inv_mass, cell_mask, weights, obs_precision, footprint):
    nk, rows, cols = right_sides.shape
    tiles, foot, obs, _ = weights.shape
    picks = tiles * foot
    n = lax.axis_size("row")
    device = lax.axis_index("row")
    ids = (footprint - (device * rows - rows)).reshape(-1)
    wanted = jnp.concatenate([ids, jnp.arange(3 * rows, dtype=jnp.int32)])
    before = jnp.concatenate(
        [jnp.arange(picks, dtype=jnp.int32), jnp.full((3 * rows,), picks, jnp.int32)]
    )
    order = jnp.arange(picks, dtype=jnp.int32)
    same = (wanted[:, None] == ids[None, :]) & (order[None, :] < before[:, None])
    last = jnp.max(jnp.where(same, order[None, :] + 1, 0), axis=1)
    index = jnp.concatenate([ids, last])

    levels = len(radices(n))
    half = cols // HALVES
    field = (rows, nk, cols)
    vmem = pl.BlockSpec(memory_space=pltpu.VMEM)
    f32, bf16 = jnp.float32, jnp.bfloat16
    solved, left = pl.pallas_call(
        functools.partial(kernel, n),
        out_shape=[jax.ShapeDtypeStruct(field, f32)] * 2,
        in_specs=[vmem]
        + [pl.BlockSpec(memory_space=pl.ANY)] * 5
        + [pl.BlockSpec(memory_space=pltpu.SMEM)],
        out_specs=[vmem] * 2,
        scratch_shapes=[
            pltpu.VMEM(weights.shape, bf16),
            pltpu.VMEM((3 * rows, nk, cols), bf16),
            pltpu.VMEM((HALVES, picks + 1, nk, half), f32),
            pltpu.VMEM((tiles, nk, obs), bf16),
            pltpu.VMEM((rows + 2, nk, cols), f32),
            pltpu.VMEM(field, f32),
            pltpu.VMEM(field, f32),
            pltpu.VMEM(field, f32),
            pltpu.VMEM((2, 2, 2, nk, cols), bf16),
            pltpu.VMEM((2, 2, 2, nk, cols), bf16),
            pltpu.VMEM((2, HALVES, 2, rows, nk, half), bf16),
            pltpu.VMEM((2, HALVES, 2, rows, nk, half), bf16),
            pltpu.VMEM(field, bf16),
            pltpu.VMEM((2,) + field, bf16),
            pltpu.VMEM((levels, RADIX, nk, 4 * nk), f32),
            pltpu.VMEM((levels, RADIX, nk // 4, 4 * nk), f32),
            pltpu.VMEM((rows, 4 * nk, cols), bf16),
            pltpu.VMEM(kappa_sq.shape, f32),
            pltpu.VMEM(inv_mass.shape, f32),
            pltpu.VMEM(cell_mask.shape, jnp.int32),
            pltpu.VMEM(obs_precision.shape, f32),
            pltpu.SemaphoreType.DMA((4,)),
            pltpu.SemaphoreType.DMA((tiles,)),
            pltpu.SemaphoreType.DMA((2, KINDS, 2)),
            pltpu.SemaphoreType.DMA((2, KINDS, 2)),
            pltpu.SemaphoreType.DMA((2, levels, RADIX)),
            pltpu.SemaphoreType.DMA((2, levels, RADIX)),
        ],
        compiler_params=pltpu.CompilerParams(
            collective_id=0, has_side_effects=True, vmem_limit_bytes=50 * 1024 * 1024
        ),
    )(
        jnp.swapaxes(right_sides, 0, 1),
        kappa_sq,
        inv_mass,
        cell_mask,
        weights,
        obs_precision,
        index,
    )
    return (jnp.swapaxes(solved, 0, 1), jnp.swapaxes(left, 0, 1))


def solution(mesh):
    placed = (
        P(None, ("grp", "row"), None),
        P(("grp", "row"), None),
        P(("grp", "row"), None),
        P(("grp", "row"), None),
        P(("grp", "row"), None, None, None),
        P(("grp", "row"), None),
        P(("grp", "row"), None),
    )
    return jax.shard_map(
        body,
        mesh=mesh,
        in_specs=placed,
        out_specs=(P(None, ("grp", "row"), None), P(None, ("grp", "row"), None)),
        check_vma=False,
    )
```

```python
import functools

import jax
import jax.numpy as jnp
from jax import lax
from jax.experimental import pallas as pl
from jax.experimental.pallas import tpu as pltpu
from jax.sharding import PartitionSpec as P

RADIX = 16
HALVES = 2
HIGHEST = lax.Precision.HIGHEST
NN = (((1,), (0,)), ((), ()))
NT = (((1,), (1,)), ((), ()))
FIELD_EDGE, HALO, INNER_EDGE, TERMS = range(4)
KINDS = TERMS + HALVES


def radices(n):
    out, stride = [], 1
    while stride < n:
        radix = min(RADIX, n // stride)
        out.append((stride, radix))
        stride *= radix
    return out


def dot(a, b, dims=NN, precision=HIGHEST):
    return lax.dot_general(a, b, dims, precision=precision, preferred_element_type=jnp.float32)


def eliminate(mats):
    k = mats[0].shape[0]
    row_id = lax.broadcasted_iota(jnp.int32, mats[0].shape, 0)
    for i in range(k):
        new = []
        for a in mats:
            row = a[i : i + 1, :] * (1.0 / a[i : i + 1, i : i + 1])
            new.append(jnp.where(row_id == i, row, a - a[:, i : i + 1] * row))
        mats = new
    return mats


def kernel(
    n,
    rhs_ref, kap_hbm, inv_hbm, mask_hbm, w_hbm, prec_hbm, idx_ref,
    sol_ref, res_ref,
    w, ext, adj, sc, masked, img, image2, dirn, es, er, ts, tr, vown, vhalo, ar0, ar1, packed,
    kap_ref, inv_ref, mask_ref, prec_ref, tsem, wsem, send_sem, recv_sem, ar_send, ar_recv,
):
    rows, nk, cols = rhs_ref.shape
    tiles, foot, obs, _ = w.shape
    picks = tiles * foot
    me = lax.axis_index("row")
    has_up, has_down = me > 0, me < n - 1
    levels = radices(n)

    half = cols // HALVES
    tables = [
        pltpu.make_async_copy(src, dst, tsem.at[i])
        for i, (src, dst) in enumerate(
            ((kap_hbm, kap_ref), (inv_hbm, inv_ref), (mask_hbm, mask_ref), (prec_hbm, prec_ref))
        )
    ]
    for c in tables:
        c.start()
    for t in range(tiles):
        pltpu.make_async_copy(w_hbm.at[t], w.at[t], wsem.at[t]).start()

    def neighbour(d):
        return {"row": lax.rem(me + (1 if d == 0 else n - 1), n)}

    def partner(stride, radix, d):
        q = lax.rem(me // stride, radix)
        return {"row": me + (lax.rem(q + d, radix) - q) * stride}

    barrier = pltpu.get_barrier_semaphore()

    def greet(device):
        pl.semaphore_signal(barrier, inc=1, device_id=device, device_id_type=pl.DeviceIdType.MESH)

    count = 0
    for stride, radix in levels:
        for d in range(1, radix):
            greet(partner(stride, radix, d))
            count += 1
    pl.when(has_down)(lambda: greet(neighbour(0)))
    pl.when(has_up)(lambda: greet(neighbour(1)))

    def copy(it, kind, d, src, dst):
        return pltpu.make_async_remote_copy(
            src_ref=src,
            dst_ref=dst,
            send_sem=send_sem.at[it, kind, d],
            recv_sem=recv_sem.at[it, kind, d],
            device_id=neighbour(d),
            device_id_type=pl.DeviceIdType.MESH,
        )

    sends = (has_down, has_up)
    receives = (has_up, has_down)

    def pair(it, kind):
        if kind == HALO:
            if it == 1:
                return tuple(copy(it, kind, d, vown, vhalo.at[d]) for d in range(2))
            own = ext.at[pl.ds(rows, rows)]
            return (
                copy(it, kind, 0, own, ext.at[pl.ds(0, rows)]),
                copy(it, kind, 1, own, ext.at[pl.ds(2 * rows, rows)]),
            )
        if kind >= TERMS:
            h = kind - TERMS
            return tuple(copy(it, kind, d, ts.at[it, h, d], tr.at[it, h, d]) for d in range(2))
        e = 0 if kind == FIELD_EDGE else 1
        return tuple(copy(it, kind, d, es.at[it, e, d], er.at[it, e, d]) for d in range(2))

    def start(it, kind):
        for d, c in enumerate(pair(it, kind)):
            pl.when(sends[d])(c.start)

    def arrive(it, kind):
        for d, c in enumerate(pair(it, kind)):
            pl.when(receives[d])(c.wait_recv)

    def drain(it, kind):
        for d, c in enumerate(pair(it, kind)):
            pl.when(sends[d])(c.wait_send)

    @pl.when(jnp.logical_not(has_up))
    def _():
        ext[pl.ds(0, rows)] = jnp.zeros((rows, nk, cols), jnp.bfloat16)
        vhalo[0] = jnp.zeros((rows, nk, cols), jnp.bfloat16)
        for it in range(2):
            for h in range(HALVES):
                tr[it, h, 0] = jnp.zeros((rows, nk, half), jnp.bfloat16)
            for e in range(2):
                er[it, e, 0] = jnp.zeros((nk, cols), jnp.bfloat16)

    @pl.when(jnp.logical_not(has_down))
    def _():
        ext[pl.ds(2 * rows, rows)] = jnp.zeros((rows, nk, cols), jnp.bfloat16)
        vhalo[1] = jnp.zeros((rows, nk, cols), jnp.bfloat16)
        for it in range(2):
            for h in range(HALVES):
                tr[it, h, 1] = jnp.zeros((rows, nk, half), jnp.bfloat16)
            for e in range(2):
                er[it, e, 1] = jnp.zeros((nk, cols), jnp.bfloat16)

    for h in range(HALVES):
        adj[h, 0] = jnp.zeros((nk, half), jnp.float32)
    for c in tables:
        c.wait()

    lane = lax.broadcasted_iota(jnp.int32, (nk, cols), 1)
    maskf = mask_ref[...].astype(jnp.float32)
    kap = kap_ref[...]
    inv = inv_ref[...]

    def at(table, r):
        return table[r : r + 1, :]

    def beside(r):
        m = masked[r + 1]
        right = jnp.where(lane == cols - 1, 0.0, pltpu.roll(m, cols - 1, 1))
        left = jnp.where(lane == 0, 0.0, pltpu.roll(m, 1, 1))
        return masked[r] + masked[r + 2] + right + left

    def stage_edges(it, e):
        for d, r in ((0, rows), (1, 1)):
            es[it, e, d] = masked[r].astype(jnp.bfloat16)

    def take_edges(it, e):
        masked[0] = er[it, e, 0].astype(jnp.float32)
        masked[rows + 1] = er[it, e, 1].astype(jnp.float32)

    def apply(it, field, out, make_halo=None):
        for r in range(rows):
            masked[r + 1] = at(maskf, r) * field[r]
            ext[rows + r] = field[r].astype(jnp.bfloat16)
        stage_edges(it, 0)
        if it == 0:
            down, up = (jnp.where(x, 1, 0) for x in (has_down, has_up))
            pl.semaphore_wait(barrier, count + down + up)
        start(it, FIELD_EDGE)
        if make_halo is None:
            start(it, HALO)
        else:
            make_halo()
        inside = list(range(1, rows - 1))
        ends = [0, rows - 1]

        def inner(r):
            value = at(kap, r) * field[r] + at(maskf, r) * (4.0 * field[r] - beside(r))
            out[r] = at(inv, r) * value

        for r in inside:
            inner(r)
        arrive(it, FIELD_EDGE)
        take_edges(it, 0)
        for r in ends:
            inner(r)
        for r in range(rows):
            masked[r + 1] = at(maskf, r) * out[r]
        stage_edges(it, 1)
        start(it, INNER_EDGE)
        if make_halo is None:
            arrive(it, HALO)

        def observe(t, carry):
            if it == 0:
                pltpu.make_async_copy(w_hbm.at[t], w.at[t], wsem.at[t]).wait()
            total = jnp.zeros((nk, obs), jnp.float32)
            for j in range(foot):
                x = ext[idx_ref[t * foot + j]]
                total += dot(x, w[t, j], NT, None)
            sc[t] = (prec_ref[pl.ds(t, 1), :] * total).astype(jnp.bfloat16)
            return carry

        lax.fori_loop(0, tiles, observe, 0, unroll=2)

        for h in range(HALVES):
            part = pl.ds(h * half, half)

            def spread(t, carry):
                for j in range(foot):
                    adj[h, 1 + t * foot + j] = dot(sc[t], w[t, j, :, part], NN, None)
                return carry

            lax.fori_loop(0, tiles, spread, 0, unroll=2)

            def link(i, carry):
                adj[h, 1 + i] = adj[h, 1 + i] + adj[h, idx_ref[picks + i]]
                return carry

            lax.fori_loop(0, picks, link, 0, unroll=4)

            def stage(r, carry):
                ts[it, h, 1, r] = adj[h, idx_ref[2 * picks + r]].astype(jnp.bfloat16)
                ts[it, h, 0, r] = adj[h, idx_ref[2 * picks + 2 * rows + r]].astype(jnp.bfloat16)
                return carry

            lax.fori_loop(0, rows, stage, 0, unroll=4)
            start(it, TERMS + h)
        arrive(it, INNER_EDGE)
        take_edges(it, 1)
        for r in range(rows):
            out[r] = at(kap, r) * out[r] + at(maskf, r) * (4.0 * out[r] - beside(r))
        for h in range(HALVES):
            part = pl.ds(h * half, half)
            arrive(it, TERMS + h)
            for r in range(rows):
                beyond = tr[it, h, 0, r].astype(jnp.float32) + tr[it, h, 1, r].astype(jnp.float32)
                out[r, :, part] += adj[h, idx_ref[2 * picks + rows + r]] + beyond
        if it == 0:
            for r in range(rows):
                vown[r] = out[r].astype(jnp.bfloat16)
        for kind in range(KINDS):
            drain(it, kind)

    def halves_of(x):
        high = x.astype(jnp.bfloat16)
        return high, (x - high.astype(jnp.float32)).astype(jnp.bfloat16)

    def pack(a, b):
        total = jnp.zeros((4 * nk, 4 * nk), jnp.float32)
        for r in range(rows):
            a_high, a_low = halves_of(a[r])
            b_high, b_low = halves_of(b[r])
            x = jnp.concatenate([a_high, b_high, a_low, b_low], axis=0)
            packed[r] = x
            total += dot(x, x, NT, None)
        total = total[: 2 * nk] + total[2 * nk :]
        return total[:, : 2 * nk] + total[:, 2 * nk :]

    def combine(coeffs):
        high, low = halves_of(coeffs)
        wide = jnp.concatenate([high, high, low], axis=1)

        def row(r):
            x = packed[r]
            return dot(wide, jnp.concatenate([x, x[: 2 * nk]], axis=0), NN, None)

        return row

    def reduce_all(which, ar, value, meanwhile=None):
        for lv, (stride, radix) in enumerate(levels):
            q = lax.rem(me // stride, radix)
            ar[lv, q] = value
            copies = [
                pltpu.make_async_remote_copy(
                    src_ref=ar.at[lv, q],
                    dst_ref=ar.at[lv, q],
                    send_sem=ar_send.at[which, lv, d],
                    recv_sem=ar_recv.at[which, lv, d],
                    device_id=partner(stride, radix, d),
                    device_id_type=pl.DeviceIdType.MESH,
                )
                for d in range(1, radix)
            ]
            for c in copies:
                c.start()
            if meanwhile is not None and lv == 0:
                meanwhile()
            for c in copies:
                c.wait_recv()
            for c in copies:
                c.wait_send()
            value = ar[lv, 0]
            for p in range(1, radix):
                value = value + ar[lv, p]
        return value

    eye = (
        lax.broadcasted_iota(jnp.int32, (nk, nk), 0) == lax.broadcasted_iota(jnp.int32, (nk, nk), 1)
    ).astype(jnp.float32)
    pad = jnp.zeros((nk, 2 * nk), jnp.float32)

    def flipped(x):
        return dot(eye, x, NT)

    apply(0, rhs_ref, img)
    total = pack(rhs_ref, img)
    total = jnp.concatenate([total[:nk], total[nk:]], axis=1)
    total = reduce_all(0, ar0, total, lambda: start(1, HALO))
    g00, g01, g10, g11 = (total[:, p * nk : (p + 1) * nk] for p in range(4))
    first, second = eliminate(
        [
            jnp.concatenate([0.5 * (g01 + g10), g00, pad], axis=1),
            jnp.concatenate([g00, eye, pad], axis=1),
        ]
    )
    step = first[:, nk : 2 * nk]
    step_t = flipped(step)
    new_gram = g00 - dot(g01, step) - dot(step_t, g10 - dot(g11, step))
    mix_t = dot(new_gram, second[:, nk : 2 * nk])
    none = jnp.zeros((nk, nk), jnp.float32)
    rows_of = combine(
        jnp.concatenate(
            [
                jnp.concatenate([step_t, none], axis=1),
                jnp.concatenate([none, step_t], axis=1),
                jnp.concatenate([mix_t, none], axis=1),
            ],
            axis=0,
        )
    )
    for r in range(rows):
        all_three = rows_of(r)
        left = rhs_ref[r] - all_three[nk : 2 * nk]
        sol_ref[r] = all_three[:nk]
        res_ref[r] = left
        dirn[r] = left + all_three[2 * nk :]

    high, low = halves_of(jnp.concatenate([mix_t, -step_t], axis=1))
    beyond_t = jnp.concatenate([high, low], axis=1)

    def beyond_direction():
        arrive(1, HALO)
        for d in range(2):
            def one(r, carry):
                x = ext[2 * rows * d + r]
                y = vhalo[d, r]
                new = dot(beyond_t, jnp.concatenate([x, y, x, y], axis=0), NN, None)
                ext[2 * rows * d + r] = (x.astype(jnp.float32) + new).astype(jnp.bfloat16)
                return carry

            lax.fori_loop(0, rows, one, 0, unroll=4)

    apply(1, dirn, image2, beyond_direction)
    total = pack(dirn, image2)
    total = 0.5 * (total[:nk, nk:] + total[nk:, :nk])
    fold = nk // 4
    total = jnp.concatenate([total[p * fold : (p + 1) * fold] for p in range(4)], axis=1)
    total = reduce_all(1, ar1, total)
    total = jnp.concatenate([total[:, p * nk : (p + 1) * nk] for p in range(4)], axis=0)
    (third,) = eliminate([jnp.concatenate([total, new_gram, pad], axis=1)])
    step_t = flipped(third[:, nk : 2 * nk])
    rows_of = combine(
        jnp.concatenate(
            [
                jnp.concatenate([step_t, none], axis=1),
                jnp.concatenate([none, step_t], axis=1),
            ],
            axis=0,
        )
    )
    for r in range(rows):
        both = rows_of(r)
        sol_ref[r] += both[:nk]
        res_ref[r] -= both[nk:]


def body(right_sides, kappa_sq, inv_mass, cell_mask, weights, obs_precision, footprint):
    nk, rows, cols = right_sides.shape
    tiles, foot, obs, _ = weights.shape
    picks = tiles * foot
    n = lax.axis_size("row")
    device = lax.axis_index("row")
    ids = (footprint - (device * rows - rows)).reshape(-1)
    wanted = jnp.concatenate([ids, jnp.arange(3 * rows, dtype=jnp.int32)])
    before = jnp.concatenate(
        [jnp.arange(picks, dtype=jnp.int32), jnp.full((3 * rows,), picks, jnp.int32)]
    )
    order = jnp.arange(picks, dtype=jnp.int32)
    same = (wanted[:, None] == ids[None, :]) & (order[None, :] < before[:, None])
    last = jnp.max(jnp.where(same, order[None, :] + 1, 0), axis=1)
    index = jnp.concatenate([ids, last])

    levels = len(radices(n))
    half = cols // HALVES
    field = (rows, nk, cols)
    vmem = pl.BlockSpec(memory_space=pltpu.VMEM)
    f32, bf16 = jnp.float32, jnp.bfloat16
    solved, left = pl.pallas_call(
        functools.partial(kernel, n),
        out_shape=[jax.ShapeDtypeStruct(field, f32)] * 2,
        in_specs=[vmem]
        + [pl.BlockSpec(memory_space=pltpu.HBM)] * 5
        + [pl.BlockSpec(memory_space=pltpu.SMEM)],
        out_specs=[vmem] * 2,
        scratch_shapes=[
            pltpu.VMEM(weights.shape, bf16),
            pltpu.VMEM((3 * rows, nk, cols), bf16),
            pltpu.VMEM((HALVES, picks + 1, nk, half), f32),
            pltpu.VMEM((tiles, nk, obs), bf16),
            pltpu.VMEM((rows + 2, nk, cols), f32),
            pltpu.VMEM(field, f32),
            pltpu.VMEM(field, f32),
            pltpu.VMEM(field, f32),
            pltpu.VMEM((2, 2, 2, nk, cols), bf16),
            pltpu.VMEM((2, 2, 2, nk, cols), bf16),
            pltpu.VMEM((2, HALVES, 2, rows, nk, half), bf16),
            pltpu.VMEM((2, HALVES, 2, rows, nk, half), bf16),
            pltpu.VMEM(field, bf16),
            pltpu.VMEM((2,) + field, bf16),
            pltpu.VMEM((levels, RADIX, nk, 4 * nk), f32),
            pltpu.VMEM((levels, RADIX, nk // 4, 4 * nk), f32),
            pltpu.VMEM((rows, 4 * nk, cols), bf16),
            pltpu.VMEM(kappa_sq.shape, f32),
            pltpu.VMEM(inv_mass.shape, f32),
            pltpu.VMEM(cell_mask.shape, jnp.int32),
            pltpu.VMEM(obs_precision.shape, f32),
            pltpu.SemaphoreType.DMA((4,)),
            pltpu.SemaphoreType.DMA((tiles,)),
            pltpu.SemaphoreType.DMA((2, KINDS, 2)),
            pltpu.SemaphoreType.DMA((2, KINDS, 2)),
            pltpu.SemaphoreType.DMA((2, levels, RADIX)),
            pltpu.SemaphoreType.DMA((2, levels, RADIX)),
        ],
        compiler_params=pltpu.CompilerParams(
            collective_id=0, has_side_effects=True, vmem_limit_bytes=50 * 1024 * 1024
        ),
    )(
        jnp.swapaxes(right_sides, 0, 1),
        kappa_sq,
        inv_mass,
        cell_mask,
        weights,
        obs_precision,
        index,
    )
    return (jnp.swapaxes(solved, 0, 1), jnp.swapaxes(left, 0, 1))


def solution(mesh):
    placed = (
        P(None, ("grp", "row"), None),
        P(("grp", "row"), None),
        P(("grp", "row"), None),
        P(("grp", "row"), None),
        P(("grp", "row"), None, None, None),
        P(("grp", "row"), None),
        P(("grp", "row"), None),
    )
    return jax.shard_map(
        body,
        mesh=mesh,
        in_specs=placed,
        out_specs=(P(None, ("grp", "row"), None), P(None, ("grp", "row"), None)),
        check_vma=False,
    )
```

```python
import functools

import jax
import jax.numpy as jnp
from jax import lax
from jax.experimental import pallas as pl
from jax.experimental.pallas import tpu as pltpu
from jax.sharding import PartitionSpec as P

RADIX = 16
HALVES = 2
HIGHEST = lax.Precision.HIGHEST
NN = (((1,), (0,)), ((), ()))
NT = (((1,), (1,)), ((), ()))
FIELD_EDGE, HALO, INNER_EDGE, TERMS = range(4)
KINDS = TERMS + HALVES


def radices(n):
    out, stride = [], 1
    while stride < n:
        radix = min(RADIX, n // stride)
        out.append((stride, radix))
        stride *= radix
    return out


def dot(a, b, dims=NN, precision=HIGHEST):
    return lax.dot_general(a, b, dims, precision=precision, preferred_element_type=jnp.float32)


def eliminate(mats):
    k = mats[0].shape[0]
    row_id = lax.broadcasted_iota(jnp.int32, mats[0].shape, 0)
    for i in range(k):
        new = []
        for a in mats:
            row = a[i : i + 1, :] * (1.0 / a[i : i + 1, i : i + 1])
            new.append(jnp.where(row_id == i, row, a - a[:, i : i + 1] * row))
        mats = new
    return mats


def kernel(
    n,
    rhs_ref, tables_ref, w_hbm, idx_ref,
    sol_ref, res_ref,
    w, ext, adj, sc, masked, img, image2, dirn, es, er, ts, tr, vown, vhalo, ar0, ar1, packed,
    wsem, send_sem, recv_sem, ar_send, ar_recv,
):
    rows, nk, cols = rhs_ref.shape
    tiles, foot, obs, _ = w.shape
    picks = tiles * foot
    me = lax.axis_index("row")
    has_up, has_down = me > 0, me < n - 1
    levels = radices(n)

    half = cols // HALVES
    for t in range(tiles):
        pltpu.make_async_copy(w_hbm.at[t], w.at[t], wsem.at[t]).start()

    def neighbour(d):
        return {"row": lax.rem(me + (1 if d == 0 else n - 1), n)}

    def partner(stride, radix, d):
        q = lax.rem(me // stride, radix)
        return {"row": me + (lax.rem(q + d, radix) - q) * stride}

    barrier = pltpu.get_barrier_semaphore()

    def greet(device):
        pl.semaphore_signal(barrier, inc=1, device_id=device, device_id_type=pl.DeviceIdType.MESH)

    count = 0
    for stride, radix in levels:
        for d in range(1, radix):
            greet(partner(stride, radix, d))
            count += 1
    pl.when(has_down)(lambda: greet(neighbour(0)))
    pl.when(has_up)(lambda: greet(neighbour(1)))

    def copy(it, kind, d, src, dst):
        return pltpu.make_async_remote_copy(
            src_ref=src,
            dst_ref=dst,
            send_sem=send_sem.at[it, kind, d],
            recv_sem=recv_sem.at[it, kind, d],
            device_id=neighbour(d),
            device_id_type=pl.DeviceIdType.MESH,
        )

    sends = (has_down, has_up)
    receives = (has_up, has_down)

    def pair(it, kind):
        if kind == HALO:
            if it == 1:
                return tuple(copy(it, kind, d, vown, vhalo.at[d]) for d in range(2))
            own = ext.at[pl.ds(rows, rows)]
            return (
                copy(it, kind, 0, own, ext.at[pl.ds(0, rows)]),
                copy(it, kind, 1, own, ext.at[pl.ds(2 * rows, rows)]),
            )
        if kind >= TERMS:
            h = kind - TERMS
            return tuple(copy(it, kind, d, ts.at[it, h, d], tr.at[it, h, d]) for d in range(2))
        e = 0 if kind == FIELD_EDGE else 1
        return tuple(copy(it, kind, d, es.at[it, e, d], er.at[it, e, d]) for d in range(2))

    def start(it, kind):
        for d, c in enumerate(pair(it, kind)):
            pl.when(sends[d])(c.start)

    def arrive(it, kind):
        for d, c in enumerate(pair(it, kind)):
            pl.when(receives[d])(c.wait_recv)

    def drain(it, kind):
        for d, c in enumerate(pair(it, kind)):
            pl.when(sends[d])(c.wait_send)

    @pl.when(jnp.logical_not(has_up))
    def _():
        ext[pl.ds(0, rows)] = jnp.zeros((rows, nk, cols), jnp.bfloat16)
        vhalo[0] = jnp.zeros((rows, nk, cols), jnp.bfloat16)
        for it in range(2):
            for h in range(HALVES):
                tr[it, h, 0] = jnp.zeros((rows, nk, half), jnp.bfloat16)
            for e in range(2):
                er[it, e, 0] = jnp.zeros((nk, cols), jnp.bfloat16)

    @pl.when(jnp.logical_not(has_down))
    def _():
        ext[pl.ds(2 * rows, rows)] = jnp.zeros((rows, nk, cols), jnp.bfloat16)
        vhalo[1] = jnp.zeros((rows, nk, cols), jnp.bfloat16)
        for it in range(2):
            for h in range(HALVES):
                tr[it, h, 1] = jnp.zeros((rows, nk, half), jnp.bfloat16)
            for e in range(2):
                er[it, e, 1] = jnp.zeros((nk, cols), jnp.bfloat16)

    for h in range(HALVES):
        adj[h, 0] = jnp.zeros((nk, half), jnp.float32)

    lane = lax.broadcasted_iota(jnp.int32, (nk, cols), 1)
    kap, inv, maskf = (tables_ref[pl.ds(p * rows, rows), :] for p in range(3))

    def at(table, r):
        return table[r : r + 1, :]

    def beside(r):
        m = masked[r + 1]
        right = jnp.where(lane == cols - 1, 0.0, pltpu.roll(m, cols - 1, 1))
        left = jnp.where(lane == 0, 0.0, pltpu.roll(m, 1, 1))
        return masked[r] + masked[r + 2] + right + left

    def stage_edges(it, e):
        for d, r in ((0, rows), (1, 1)):
            es[it, e, d] = masked[r].astype(jnp.bfloat16)

    def take_edges(it, e):
        masked[0] = er[it, e, 0].astype(jnp.float32)
        masked[rows + 1] = er[it, e, 1].astype(jnp.float32)

    def apply(it, field, out, make_halo=None):
        for r in range(rows):
            masked[r + 1] = at(maskf, r) * field[r]
            ext[rows + r] = field[r].astype(jnp.bfloat16)
        stage_edges(it, 0)
        if it == 0:
            down, up = (jnp.where(x, 1, 0) for x in (has_down, has_up))
            pl.semaphore_wait(barrier, count + down + up)
        start(it, FIELD_EDGE)
        if make_halo is None:
            start(it, HALO)
        else:
            make_halo()
        inside = list(range(1, rows - 1))
        ends = [0, rows - 1]

        def inner(r):
            value = at(kap, r) * field[r] + at(maskf, r) * (4.0 * field[r] - beside(r))
            out[r] = at(inv, r) * value

        for r in inside:
            inner(r)
        arrive(it, FIELD_EDGE)
        take_edges(it, 0)
        for r in ends:
            inner(r)
        for r in range(rows):
            masked[r + 1] = at(maskf, r) * out[r]
        stage_edges(it, 1)
        start(it, INNER_EDGE)
        if make_halo is None:
            arrive(it, HALO)

        def observe(t, carry):
            if it == 0:
                pltpu.make_async_copy(w_hbm.at[t], w.at[t], wsem.at[t]).wait()
            total = jnp.zeros((nk, obs), jnp.float32)
            for j in range(foot):
                x = ext[idx_ref[t * foot + j]]
                total += dot(x, w[t, j], NT, None)
            sc[t] = (tables_ref[pl.ds(3 * rows + t, 1), :][:, :obs] * total).astype(jnp.bfloat16)
            return carry

        lax.fori_loop(0, tiles, observe, 0, unroll=2)

        for h in range(HALVES):
            part = pl.ds(h * half, half)

            def spread(t, carry):
                for j in range(foot):
                    adj[h, 1 + t * foot + j] = dot(sc[t], w[t, j, :, part], NN, None)
                return carry

            lax.fori_loop(0, tiles, spread, 0, unroll=2)

            def link(i, carry):
                adj[h, 1 + i] = adj[h, 1 + i] + adj[h, idx_ref[picks + i]]
                return carry

            lax.fori_loop(0, picks, link, 0, unroll=4)

            def stage(r, carry):
                ts[it, h, 1, r] = adj[h, idx_ref[2 * picks + r]].astype(jnp.bfloat16)
                ts[it, h, 0, r] = adj[h, idx_ref[2 * picks + 2 * rows + r]].astype(jnp.bfloat16)
                return carry

            lax.fori_loop(0, rows, stage, 0, unroll=4)
            start(it, TERMS + h)
        arrive(it, INNER_EDGE)
        take_edges(it, 1)
        for r in range(rows):
            out[r] = at(kap, r) * out[r] + at(maskf, r) * (4.0 * out[r] - beside(r))
        for h in range(HALVES):
            part = pl.ds(h * half, half)
            arrive(it, TERMS + h)
            for r in range(rows):
                beyond = tr[it, h, 0, r].astype(jnp.float32) + tr[it, h, 1, r].astype(jnp.float32)
                out[r, :, part] += adj[h, idx_ref[2 * picks + rows + r]] + beyond
        if it == 0:
            for r in range(rows):
                vown[r] = out[r].astype(jnp.bfloat16)
        for kind in range(KINDS):
            drain(it, kind)

    def halves_of(x):
        high = x.astype(jnp.bfloat16)
        return high, (x - high.astype(jnp.float32)).astype(jnp.bfloat16)

    def pack(a, b):
        total = jnp.zeros((4 * nk, 4 * nk), jnp.float32)
        for r in range(rows):
            a_high, a_low = halves_of(a[r])
            b_high, b_low = halves_of(b[r])
            x = jnp.concatenate([a_high, b_high, a_low, b_low], axis=0)
            packed[r] = x
            total += dot(x, x, NT, None)
        total = total[: 2 * nk] + total[2 * nk :]
        return total[:, : 2 * nk] + total[:, 2 * nk :]

    def combine(coeffs):
        high, low = halves_of(coeffs)
        wide = jnp.concatenate([high, high, low], axis=1)

        def row(r):
            x = packed[r]
            return dot(wide, jnp.concatenate([x, x[: 2 * nk]], axis=0), NN, None)

        return row

    def reduce_all(which, ar, value, meanwhile=None):
        for lv, (stride, radix) in enumerate(levels):
            q = lax.rem(me // stride, radix)
            ar[lv, q] = value
            copies = [
                pltpu.make_async_remote_copy(
                    src_ref=ar.at[lv, q],
                    dst_ref=ar.at[lv, q],
                    send_sem=ar_send.at[which, lv, d],
                    recv_sem=ar_recv.at[which, lv, d],
                    device_id=partner(stride, radix, d),
                    device_id_type=pl.DeviceIdType.MESH,
                )
                for d in range(1, radix)
            ]
            for c in copies:
                c.start()
            if meanwhile is not None and lv == 0:
                meanwhile()
            for c in copies:
                c.wait_recv()
            for c in copies:
                c.wait_send()
            value = ar[lv, 0]
            for p in range(1, radix):
                value = value + ar[lv, p]
        return value

    eye = (
        lax.broadcasted_iota(jnp.int32, (nk, nk), 0) == lax.broadcasted_iota(jnp.int32, (nk, nk), 1)
    ).astype(jnp.float32)
    pad = jnp.zeros((nk, 2 * nk), jnp.float32)

    def flipped(x):
        return dot(eye, x, NT)

    apply(0, rhs_ref, img)
    total = pack(rhs_ref, img)
    total = jnp.concatenate([total[:nk], total[nk:]], axis=1)
    total = reduce_all(0, ar0, total, lambda: start(1, HALO))
    g00, g01, g10, g11 = (total[:, p * nk : (p + 1) * nk] for p in range(4))
    first, second = eliminate(
        [
            jnp.concatenate([0.5 * (g01 + g10), g00, pad], axis=1),
            jnp.concatenate([g00, eye, pad], axis=1),
        ]
    )
    step = first[:, nk : 2 * nk]
    step_t = flipped(step)
    new_gram = g00 - dot(g01, step) - dot(step_t, g10 - dot(g11, step))
    mix_t = dot(new_gram, second[:, nk : 2 * nk])
    none = jnp.zeros((nk, nk), jnp.float32)
    rows_of = combine(
        jnp.concatenate(
            [
                jnp.concatenate([step_t, none], axis=1),
                jnp.concatenate([none, step_t], axis=1),
                jnp.concatenate([mix_t, none], axis=1),
            ],
            axis=0,
        )
    )
    for r in range(rows):
        all_three = rows_of(r)
        left = rhs_ref[r] - all_three[nk : 2 * nk]
        sol_ref[r] = all_three[:nk]
        res_ref[r] = left
        dirn[r] = left + all_three[2 * nk :]

    high, low = halves_of(jnp.concatenate([mix_t, -step_t], axis=1))
    beyond_t = jnp.concatenate([high, low], axis=1)

    def beyond_direction():
        arrive(1, HALO)
        for d in range(2):
            def one(r, carry):
                x = ext[2 * rows * d + r]
                y = vhalo[d, r]
                new = dot(beyond_t, jnp.concatenate([x, y, x, y], axis=0), NN, None)
                ext[2 * rows * d + r] = (x.astype(jnp.float32) + new).astype(jnp.bfloat16)
                return carry

            lax.fori_loop(0, rows, one, 0, unroll=4)

    apply(1, dirn, image2, beyond_direction)
    total = pack(dirn, image2)
    total = 0.5 * (total[:nk, nk:] + total[nk:, :nk])
    fold = nk // 4
    total = jnp.concatenate([total[p * fold : (p + 1) * fold] for p in range(4)], axis=1)
    total = reduce_all(1, ar1, total)
    total = jnp.concatenate([total[:, p * nk : (p + 1) * nk] for p in range(4)], axis=0)
    (third,) = eliminate([jnp.concatenate([total, new_gram, pad], axis=1)])
    step_t = flipped(third[:, nk : 2 * nk])
    rows_of = combine(
        jnp.concatenate(
            [
                jnp.concatenate([step_t, none], axis=1),
                jnp.concatenate([none, step_t], axis=1),
            ],
            axis=0,
        )
    )
    for r in range(rows):
        both = rows_of(r)
        sol_ref[r] += both[:nk]
        res_ref[r] -= both[nk:]


def body(right_sides, kappa_sq, inv_mass, cell_mask, weights, obs_precision, footprint):
    nk, rows, cols = right_sides.shape
    tiles, foot, obs, _ = weights.shape
    picks = tiles * foot
    n = lax.axis_size("row")
    device = lax.axis_index("row")
    ids = (footprint - (device * rows - rows)).reshape(-1)
    wanted = jnp.concatenate([ids, jnp.arange(3 * rows, dtype=jnp.int32)])
    before = jnp.concatenate(
        [jnp.arange(picks, dtype=jnp.int32), jnp.full((3 * rows,), picks, jnp.int32)]
    )
    order = jnp.arange(picks, dtype=jnp.int32)
    same = (wanted[:, None] == ids[None, :]) & (order[None, :] < before[:, None])
    last = jnp.max(jnp.where(same, order[None, :] + 1, 0), axis=1)
    index = jnp.concatenate([ids, last])

    tables = jnp.concatenate(
        [
            kappa_sq,
            inv_mass,
            cell_mask.astype(jnp.float32),
            jnp.pad(obs_precision, ((0, 0), (0, cols - obs))),
        ],
        axis=0,
    )
    levels = len(radices(n))
    half = cols // HALVES
    field = (rows, nk, cols)
    vmem = pl.BlockSpec(memory_space=pltpu.VMEM)
    f32, bf16 = jnp.float32, jnp.bfloat16
    solved, left = pl.pallas_call(
        functools.partial(kernel, n),
        out_shape=[jax.ShapeDtypeStruct(field, f32)] * 2,
        in_specs=[vmem]
        + [vmem, pl.BlockSpec(memory_space=pltpu.HBM)]
        + [pl.BlockSpec(memory_space=pltpu.SMEM)],
        out_specs=[vmem] * 2,
        scratch_shapes=[
            pltpu.VMEM(weights.shape, bf16),
            pltpu.VMEM((3 * rows, nk, cols), bf16),
            pltpu.VMEM((HALVES, picks + 1, nk, half), f32),
            pltpu.VMEM((tiles, nk, obs), bf16),
            pltpu.VMEM((rows + 2, nk, cols), f32),
            pltpu.VMEM(field, f32),
            pltpu.VMEM(field, f32),
            pltpu.VMEM(field, f32),
            pltpu.VMEM((2, 2, 2, nk, cols), bf16),
            pltpu.VMEM((2, 2, 2, nk, cols), bf16),
            pltpu.VMEM((2, HALVES, 2, rows, nk, half), bf16),
            pltpu.VMEM((2, HALVES, 2, rows, nk, half), bf16),
            pltpu.VMEM(field, bf16),
            pltpu.VMEM((2,) + field, bf16),
            pltpu.VMEM((levels, RADIX, nk, 4 * nk), f32),
            pltpu.VMEM((levels, RADIX, nk // 4, 4 * nk), f32),
            pltpu.VMEM((rows, 4 * nk, cols), bf16),
            pltpu.SemaphoreType.DMA((tiles,)),
            pltpu.SemaphoreType.DMA((2, KINDS, 2)),
            pltpu.SemaphoreType.DMA((2, KINDS, 2)),
            pltpu.SemaphoreType.DMA((2, levels, RADIX)),
            pltpu.SemaphoreType.DMA((2, levels, RADIX)),
        ],
        compiler_params=pltpu.CompilerParams(
            collective_id=0, has_side_effects=True, vmem_limit_bytes=50 * 1024 * 1024
        ),
    )(
        jnp.swapaxes(right_sides, 0, 1),
        tables,
        weights,
        index,
    )
    return (jnp.swapaxes(solved, 0, 1), jnp.swapaxes(left, 0, 1))


def solution(mesh):
    placed = (
        P(None, ("grp", "row"), None),
        P(("grp", "row"), None),
        P(("grp", "row"), None),
        P(("grp", "row"), None),
        P(("grp", "row"), None, None, None),
        P(("grp", "row"), None),
        P(("grp", "row"), None),
    )
    return jax.shard_map(
        body,
        mesh=mesh,
        in_specs=placed,
        out_specs=(P(None, ("grp", "row"), None), P(None, ("grp", "row"), None)),
        check_vma=False,
    )
```
